32 devices in a mesh: gx: 4 (over z), gy: 4 (over y, x), sa: 2 (over core).
Axes of the slice: x: 2, y: 2, z: 4, core: 2. Of those that a mesh axis runs over, the one named last changes fastest.
Arguments:
- field: float32 [33, 16, 168, 256], P(None, 'gx', 'gy', 'sa'), as said below
- start: float32 [33, 16], replicated, may hold values from -1 to 1
Outputs:
- basis: float32 [33, 16], replicated
- gram_two: float32 [168, 168], P('gy', ('gx', 'sa'))
The draws below stay inside these ranges and needn't reach their ends.
Inputs may be any that keep to these rules, and one draw needn't show every extreme that they name: `field`: every entry is finite; species differ in scale.
All inputs are finite; a program needn't handle non-finite values.
Results may differ from the reference program's by a relative error of at most 0.0003.
Values sent between devices are 32-bit elements; how exact they have to be, the bound alone decides.
No kernel may reach another device: no remote copies, remote signals or barrier semaphores. Data moves between devices by JAX's collectives and lax.ppermute only.
A program may use at most 128 MiB of HBM per device.

```python
import jax
import jax.numpy as jnp
from jax import lax

S = 33
R = 16
ITERS = 4
NX = 16
NY = 168
NZ = 256


def draw_field(key, part):
    keys = jax.random.split(key, 5)
    shape = (S, NX, NY, NZ)
    mode_count = 48
    species_scale = jnp.exp(jax.random.uniform(keys[0], (S, 1, 1, 1), jnp.float32) * jnp.log(10.0))
    position = jnp.arange(NX, dtype=jnp.float32).reshape(1, NX, 1, 1)
    rising = jnp.sqrt(1.0 + 2.0 * position / max(NX - 1, 1))
    weight_y = jax.random.uniform(keys[1], (1, 1, NY, 1), jnp.float32, 0.5, 1.5)
    profiles = jax.random.normal(keys[4], (mode_count, NY), jnp.float32)
    noise = jax.random.normal(keys[2], shape, jnp.float32)
    mode_loads = jax.random.normal(keys[3], (S, NX, mode_count, NZ), jnp.float32)
    common = jnp.einsum('sxmz,my->sxyz', mode_loads, profiles, precision=lax.Precision.HIGHEST) / jnp.sqrt(float(mode_count))
    return species_scale * rising * (noise + common * weight_y)


def scatter_about(own_key, extent, deviation, reach, kind=jnp.bfloat16):
    drawn = jax.random.normal(own_key, extent, jnp.float32) * deviation
    return jnp.minimum(jnp.maximum(drawn, -reach), reach).astype(kind)


def setup_inputs(seed: int = 0) -> dict:
    seeds = jax.random.split(jax.random.key(seed), 3)
    field = draw_field(jax.random.fold_in(seeds[2], 71), 0)
    start = scatter_about(seeds[1], (S, R), S ** -0.5, 1.0, jnp.float32)
    return {"field": field, "start": start}


HIGH = lax.Precision.HIGHEST

def orth(block):
    inner = jnp.dot(block.T.astype(jnp.float32), block.astype(jnp.float32), precision=HIGH, preferred_element_type=jnp.float32)
    lower = jnp.linalg.cholesky(inner)
    return jax.scipy.linalg.solve_triangular(lower, block.T, lower=True).T

def leading(gram, start):
    basis = orth(orth(start))
    for step in range(ITERS):
        basis = orth(orth(jnp.dot(gram.astype(jnp.float32), basis.astype(jnp.float32), precision=HIGH, preferred_element_type=jnp.float32)))
    return basis

def reference(field, start):
    flat = field.reshape(S, -1)
    species_gram = jnp.dot(flat.astype(jnp.float32), flat.T.astype(jnp.float32), precision=HIGH, preferred_element_type=jnp.float32) / (NX * NY * NZ)
    basis = leading(species_gram, start)
    core = jnp.einsum('sr,sxyz->rxyz', basis, field, precision=HIGH)
    gram_two = jnp.einsum('rxiz,rxjz->ij', core, core, precision=HIGH) / (R * NX * NZ)
    return (basis, gram_two)
```

```python
import functools
import math

import jax
import jax.numpy as jnp
from jax import lax
from jax.experimental import pallas as pl
from jax.experimental.pallas import tpu as pltpu
from jax.sharding import PartitionSpec as P

ITERS = 4
LANES = 128
ROWS = 8
HIGH = lax.Precision.HIGHEST
BY_LAST = (((1,), (1,)), ((), ()))
ALL = ("gx", "gy", "sa")


def up(value, step):
    return -(-value // step) * step


def split(value):
    high = value.astype(jnp.bfloat16)
    low = (value - high.astype(jnp.float32)).astype(jnp.bfloat16)
    return high, low


def dot32(left, right, dims):
    return lax.dot_general(left, right, dims, preferred_element_type=jnp.float32)


def triangle(species):
    places, at = [], 0
    for top in range(0, species, ROWS):
        places.append((top, at))
        at += species - top
    return places, at


def gram_kernel(field_ref, out_ref, total):
    step = pl.program_id(0)
    species, _, lines, cells = field_ref.shape
    flat = jnp.concatenate([field_ref[:, 0, y, :] for y in range(lines)], axis=1)
    part = lax.dot_general(flat, flat, BY_LAST, precision=HIGH, preferred_element_type=jnp.float32)

    @pl.when(step == 0)
    def _():
        total[...] = jnp.zeros_like(total)

    total[:species, :species] += part

    @pl.when(step == pl.num_programs(0) - 1)
    def _():
        lane = lax.broadcasted_iota(jnp.int32, (ROWS, LANES), 1)
        tile = jnp.zeros((ROWS, LANES), jnp.float32)
        for top, at in triangle(species)[0]:
            rows = pltpu.roll(total[top : top + ROWS, :], (at - top) % LANES, 1)
            tile = jnp.where((lane >= at) & (lane < at + species - top), rows, tile)
        out_ref[...] = jnp.broadcast_to(tile[None], out_ref.shape)


def gram_tiles(field, devices):
    species, cells_x, lines, cells = field.shape
    return pl.pallas_call(
        gram_kernel,
        grid=(cells_x,),
        in_specs=[pl.BlockSpec((species, 1, lines, cells), lambda i: (0, i, 0, 0))],
        out_specs=pl.BlockSpec((devices, ROWS, LANES), lambda i: (0, 0, 0)),
        out_shape=jax.ShapeDtypeStruct((devices, ROWS, LANES), jnp.float32),
        scratch_shapes=[pltpu.VMEM((up(species, ROWS), LANES), jnp.float32)],
        compiler_params=pltpu.CompilerParams(vmem_limit_bytes=40 * 2**20),
        name="gram_tiles",
    )(field)


def orth(rows):
    ranks = rows.shape[0]
    inner = lax.dot_general(rows, rows, BY_LAST, precision=HIGH, preferred_element_type=jnp.float32)
    columns = [jnp.broadcast_to(inner[:, k : k + 1], (ranks, LANES)) for k in range(ranks)]
    index = lax.broadcasted_iota(jnp.int32, (ranks, LANES), 0)
    pivots = jnp.ones((ranks, LANES), jnp.float32)
    for k in range(ranks):
        pivot = columns[k][k : k + 1, :]
        factor = jnp.where(index > k, columns[k] * (1.0 / pivot), 0.0)
        pivots = jnp.where(index == k, pivot, pivots)
        for j in range(k + 1, ranks):
            columns[j] = columns[j] - factor * columns[j][k : k + 1, :]
        rows = rows - factor * rows[k : k + 1, :]
    return rows * lax.rsqrt(pivots)


def start_kernel(start_ref, out_ref):
    out_ref[...] = orth(orth(start_ref[...]))


def basis_kernel(species, scale, tiles_ref, start_ref, rows_ref, basis_ref):
    tile = jnp.sum(tiles_ref[...], axis=0) * scale
    places, _ = triangle(species)
    parts = [pltpu.roll(tile, (top - at) % LANES, 1) for top, at in places]
    parts += [jnp.zeros((ROWS, LANES), jnp.float32)] * (LANES // ROWS - len(parts))
    upper = jnp.concatenate(parts, axis=0)
    row = lax.broadcasted_iota(jnp.int32, (LANES, LANES), 0)
    column = lax.broadcasted_iota(jnp.int32, (LANES, LANES), 1)
    gram = jnp.where(column >= row // ROWS * ROWS, upper, upper.T)
    gram = jnp.where((row < species) & (column < species), gram, 0.0)
    rows = start_ref[...]
    for _ in range(ITERS):
        rows = orth(orth(jnp.dot(rows, gram, precision=HIGH, preferred_element_type=jnp.float32)))
    rows_ref[...] = rows
    basis_ref[...] = rows.T[:species, :]


def whole_call(kernel, out_shape, name, *args):
    return pl.pallas_call(
        kernel,
        out_shape=out_shape,
        compiler_params=pltpu.CompilerParams(vmem_limit_bytes=40 * 2**20),
        name=name,
    )(*args)


def core_kernel(count, me_ref, rows_ref, field_ref, *out_refs):
    del me_ref
    step = pl.program_id(0)
    species, _, lines, cells = field_ref.shape
    ranks = rows_ref.shape[0]
    flat = jnp.concatenate([field_ref[:, 0, y, :] for y in range(lines)], axis=1)
    high, low = split(flat)
    basis_high, basis_low = split(rows_ref[:, :species])
    dims = (((1,), (0,)), ((), ()))
    both = dot32(jnp.concatenate([basis_high, basis_low], axis=0), high, dims)
    core = both[:ranks] + both[ranks:] + dot32(basis_high, low, dims)
    for k in range(count):

        @pl.when(step == k)
        def _(k=k):
            for y in range(lines):
                out_refs[k][y] = core[:, y * cells : (y + 1) * cells]


def core_pieces(rows, field, me, count):
    species, cells_x, lines, cells = field.shape
    ranks = rows.shape[0]
    piece = (lines, ranks, cells)
    return pl.pallas_call(
        functools.partial(core_kernel, count),
        grid_spec=pltpu.PrefetchScalarGridSpec(
            num_scalar_prefetch=1,
            grid=(count,),
            in_specs=[
                pl.BlockSpec(rows.shape, lambda i, me: (0, 0)),
                pl.BlockSpec((species, 1, lines, cells), lambda i, me: (0, me[i], 0, 0)),
            ],
            out_specs=[pl.BlockSpec(piece, lambda i, me: (0, 0, 0))] * count,
        ),
        out_shape=[jax.ShapeDtypeStruct(piece, jnp.float32)] * count,
        compiler_params=pltpu.CompilerParams(vmem_limit_bytes=40 * 2**20),
        name="core_pieces",
    )(me, rows, field)


def packing(lines, columns):
    groups = LANES // lines
    deep = -(-columns // groups)
    return groups, deep, up(deep, ROWS)


def line_kernel(axes, order_ref, *refs):
    n_gx, n_gy, n_sa = axes
    pieces, (out_ref, high_ref, low_ref, gram_ref) = refs[:n_gy], refs[n_gy:]
    lines, ranks, cells = pieces[0].shape
    pitch = high_ref.shape[0] // n_gy
    high_ref[...] = jnp.zeros_like(high_ref)
    low_ref[...] = jnp.zeros_like(low_ref)
    for k in range(n_gy):
        at = pl.multiple_of(order_ref[k] * pitch, pitch)
        for r in range(ranks):
            block = jnp.concatenate(
                [pieces[k][:, r, :], jnp.zeros((pitch - lines, cells), jnp.float32)], axis=0
            )
            high, low = split(block)
            high_ref[pl.ds(at, pitch), r * cells : (r + 1) * cells] = high
            low_ref[pl.ds(at, pitch), r * cells : (r + 1) * cells] = low
    size = n_gy * pitch
    gram_ref[...] = jnp.zeros_like(gram_ref)
    gram_ref[:size, :size] = dot32(high_ref[...], low_ref[...], BY_LAST)
    cross = gram_ref[:size, :size]
    gram_ref[:size, :size] = dot32(high_ref[...], high_ref[...], BY_LAST) + cross + cross.T
    wide = gram_ref.shape[1]
    columns = lines * n_gy // (n_gx * n_sa)
    groups, deep, tall = packing(lines, columns)
    lane = lax.broadcasted_iota(jnp.int32, (tall, LANES), 1)
    for c in range(n_gx * n_sa):
        first = c * columns
        base = first // lines * pitch + first % lines
        bands = [gram_ref[base + g * deep : base + g * deep + tall, :] for g in range(groups)]
        for i in range(n_gy):
            tile = jnp.zeros((tall, LANES), jnp.float32)
            for g in range(groups):
                moved = pltpu.roll(bands[g], (g * lines - i * pitch) % wide, 1)[:, :LANES]
                tile = jnp.where((lane >= g * lines) & (lane < (g + 1) * lines), moved, tile)
            out_ref[((c // n_sa) * n_gy + i) * n_sa + c % n_sa] = tile


def line_tiles(pieces, order, axes):
    n_gx, n_gy, n_sa = axes
    lines, ranks, cells = pieces[0].shape
    pitch = up(lines, 16)
    columns = lines * n_gy // (n_gx * n_sa)
    _, _, tall = packing(lines, columns)
    size = n_gy * pitch
    return pl.pallas_call(
        functools.partial(line_kernel, axes),
        in_specs=[pl.BlockSpec(memory_space=pltpu.SMEM)]
        + [pl.BlockSpec(memory_space=pltpu.VMEM)] * n_gy,
        out_specs=pl.BlockSpec(memory_space=pltpu.VMEM),
        out_shape=jax.ShapeDtypeStruct((n_gx * n_gy * n_sa, tall, LANES), jnp.float32),
        scratch_shapes=[
            pltpu.VMEM((size, ranks * cells), jnp.bfloat16),
            pltpu.VMEM((size, ranks * cells), jnp.bfloat16),
            pltpu.VMEM((size + tall, up(size, LANES)), jnp.float32),
        ],
        compiler_params=pltpu.CompilerParams(vmem_limit_bytes=40 * 2**20),
        name="line_tiles",
    )(order, *pieces)


def block_kernel(scale, tiles_ref, out_ref):
    lines, columns = out_ref.shape
    groups, deep, tall = packing(lines, columns)
    tile = jnp.sum(tiles_ref[...], axis=0) * scale
    parts = [tile if g == 0 else pltpu.roll(tile, LANES - g * lines, 1) for g in range(groups)]
    high = groups * tall
    stack = jnp.concatenate(parts + [jnp.zeros((LANES - high, LANES), jnp.float32)], axis=0).T
    lane = lax.broadcasted_iota(jnp.int32, (LANES, LANES), 1)
    out = stack
    for g in range(1, groups):
        moved = pltpu.roll(stack, LANES - g * (tall - deep), 1)
        out = jnp.where(lane >= g * deep, moved, out)
    out_ref[...] = out[:lines, :columns]


def exchange(piece, axis, size, k):
    if size & (size - 1):
        raise ValueError("axis size")
    return lax.ppermute(piece, axis, [(a, a ^ k) for a in range(size)])


def on_device(field, start):
    species, cells_x, lines, cells_z = field.shape
    ranks = start.shape[1]
    n_gx, n_gy, n_sa = lax.axis_size("gx"), lax.axis_size("gy"), lax.axis_size("sa")
    devices = n_gx * n_gy * n_sa
    total_x, total_y, total_z = cells_x * n_gx, lines * n_gy, cells_z * n_sa
    columns = total_y // (n_gx * n_sa)
    me = lax.axis_index("gy")
    order = jnp.bitwise_xor(jnp.arange(n_gy, dtype=jnp.int32), me.astype(jnp.int32))

    first = whole_call(
        start_kernel,
        jax.ShapeDtypeStruct((ranks, LANES), jnp.float32),
        "start_rows",
        jnp.pad(start.T, ((0, 0), (0, LANES - species))),
    )
    tiles = lax.all_to_all(gram_tiles(field, devices), ALL, 0, 0, tiled=True)
    rows, basis = whole_call(
        functools.partial(basis_kernel, species, 1.0 / (total_x * total_y * total_z)),
        [
            jax.ShapeDtypeStruct((ranks, LANES), jnp.float32),
            jax.ShapeDtypeStruct((species, ranks), jnp.float32),
        ],
        "basis_rows",
        tiles,
        first,
    )
    scale = 1.0 / (ranks * total_x * total_z)
    parts_x = math.gcd(n_gy, cells_x)
    parts_z = n_gy // parts_x
    if parts_x == cells_x and parts_z == 1:
        pieces = core_pieces(rows, field, order, n_gy)
        deep = cells_z
    else:
        wide_x, wide_z = cells_x // parts_x, cells_z // parts_z
        core = jnp.einsum("rs,sxyz->yrxz", rows[:, :species], field, precision=HIGH)
        pieces = []
        for k in range(n_gy):
            at = jnp.bitwise_xor(me, k)
            cut = lax.dynamic_slice(
                core,
                (0, 0, at // parts_z * wide_x, at % parts_z * wide_z),
                (lines, ranks, wide_x, wide_z),
            )
            pieces.append(cut.reshape(lines, -1, LANES))
    pieces = [pieces[0]] + [exchange(pieces[k], "gy", n_gy, k) for k in range(1, n_gy)]
    blocks = lax.all_to_all(line_tiles(pieces, order, (n_gx, n_gy, n_sa)), ALL, 0, 0, tiled=True)
    block = whole_call(
        functools.partial(block_kernel, scale),
        jax.ShapeDtypeStruct((lines, columns), jnp.float32),
        "own_block",
        blocks,
    )
    return (basis, block)


def solution(mesh):
    in_specs = (P(None, "gx", "gy", "sa"), P())
    out_specs = (P(), P("gy", ("gx", "sa")))
    return jax.shard_map(
        on_device, mesh=mesh, in_specs=in_specs, out_specs=out_specs, check_vma=False
    )
```

```python
import functools
import math

import jax
import jax.numpy as jnp
from jax import lax
from jax.experimental import pallas as pl
from jax.experimental.pallas import tpu as pltpu
from jax.sharding import PartitionSpec as P

ITERS = 4
LANES = 128
ROWS = 8
HALF_ROWS = 16
HIGH = lax.Precision.HIGHEST
BY_LAST = (((1,), (1,)), ((), ()))
PLAIN = (((1,), (0,)), ((), ()))
ALL = ("gx", "gy", "sa")
VMEM = pl.BlockSpec(memory_space=pltpu.VMEM)
ANY = pl.BlockSpec(memory_space=pl.ANY)
SMALL = pltpu.CompilerParams(vmem_limit_bytes=4 * 2**20)
PARAMS = pltpu.CompilerParams(vmem_limit_bytes=16 * 2**20)
MIDDLE = pltpu.CompilerParams(vmem_limit_bytes=32 * 2**20)
LARGE = pltpu.CompilerParams(vmem_limit_bytes=61 * 2**20)


def lasting(time):
    return pl.CostEstimate(flops=0, bytes_accessed=int(time * 3.5e6), transcendentals=0)


def partner(k):
    return jnp.bitwise_xor(lax.axis_index("gy"), k)


def up(value, step):
    return -(-value // step) * step


def split(value):
    high = value.astype(jnp.bfloat16)
    low = (value - high.astype(jnp.float32)).astype(jnp.bfloat16)
    return high, low


def dot32(left, right, dims):
    return lax.dot_general(left, right, dims, preferred_element_type=jnp.float32)


def triangle(species):
    places, at = [], 0
    for top in range(0, species, ROWS):
        places.append((top, at))
        at += species - top
    return places


def stacked(rows, pitch):
    species, lines, cells = rows.shape
    high, low = split(rows.reshape(species, lines * cells))
    blank = jnp.zeros((pitch - species, lines * cells), jnp.bfloat16)
    return jnp.concatenate([high, blank, low, blank], axis=0)


def gram_kernel(cuts, cells_x, field_ref, tiles_ref, *refs):
    early_refs, (buffer, early, total, sems) = refs[:-4], refs[-4:]
    species = field_ref.shape[0]
    pitch = up(species, HALF_ROWS)
    spans = [slice(top, end) for top, end in zip(cuts[:-1], cuts[1:], strict=True)]
    copies = [
        pltpu.make_async_copy(field_ref.at[:, span, :], buffer.at[:, span, :], sems.at[i])
        for i, span in enumerate(spans)
    ]
    for copy in copies:
        copy.start()
    total[...] = jnp.zeros_like(total)
    sends = [
        pltpu.make_async_copy(early.at[k], ref, sems.at[len(copies) + k])
        for k, ref in enumerate(early_refs)
    ]
    for i, (copy, span) in enumerate(zip(copies, spans, strict=True)):
        copy.wait()
        for k, send in enumerate(sends if i == 0 else ()):
            early[k] = buffer[:, pl.ds(partner(partners(len(sends))[k]), early.shape[2], stride=cells_x), :]
            send.start()
        both = stacked(buffer[:, span, :], pitch)
        total[: 2 * pitch, : 2 * pitch] += dot32(both, both, BY_LAST)
    upper = total[:pitch, :] + total[pitch : 2 * pitch, :]
    upper = upper + pltpu.roll(upper, LANES - pitch, 1)
    lane = lax.broadcasted_iota(jnp.int32, (ROWS, LANES), 1)
    tile = jnp.zeros((ROWS, LANES), jnp.float32)
    for top, at in triangle(species):
        moved = pltpu.roll(upper[top : top + ROWS, :], (at - top) % LANES, 1)
        tile = jnp.where((lane >= at) & (lane < at + species - top), moved, tile)
    tiles_ref[...] = jnp.broadcast_to(tile[None], tiles_ref.shape)
    for send in sends:
        send.wait()


def by_rows(field):
    species, cells_x, lines, cells = field.shape
    return field.transpose(0, 2, 1, 3).reshape(species, lines * cells_x, cells)


def gram_tiles(field, devices, early, count):
    species, cells_x, lines, cells = field.shape
    rows = lines * cells_x
    pitch = up(species, HALF_ROWS)
    cuts = (0, max(up(rows * 2 // 5, ROWS), early * cells_x), up(rows * 3 // 4, ROWS), rows)
    return pl.pallas_call(
        functools.partial(gram_kernel, cuts, cells_x),
        in_specs=[ANY],
        out_specs=[VMEM] + [ANY] * count,
        out_shape=[jax.ShapeDtypeStruct((devices, ROWS, LANES), jnp.float32)]
        + [jax.ShapeDtypeStruct((species, early, cells), jnp.float32)] * count,
        scratch_shapes=[
            pltpu.VMEM((species, rows, cells), jnp.float32),
            pltpu.VMEM((max(count, 1), species, max(early, ROWS), cells), jnp.float32),
            pltpu.VMEM((up(2 * pitch, LANES), LANES), jnp.float32),
            pltpu.SemaphoreType.DMA((len(cuts) - 1 + count,)),
        ],
        compiler_params=LARGE,
        name="gram_tiles",
    )(by_rows(field))


def orth(rows):
    ranks = rows.shape[0]
    inner = lax.dot_general(rows, rows, BY_LAST, precision=HIGH, preferred_element_type=jnp.float32)
    columns = [jnp.broadcast_to(inner[:, k : k + 1], (ranks, LANES)) for k in range(ranks)]
    index = lax.broadcasted_iota(jnp.int32, (ranks, LANES), 0)
    pivots = jnp.ones((ranks, LANES), jnp.float32)
    for k in range(ranks):
        pivot = columns[k][k : k + 1, :]
        factor = jnp.where(index > k, columns[k] * (1.0 / pivot), 0.0)
        pivots = jnp.where(index == k, pivot, pivots)
        for j in range(k + 1, ranks):
            columns[j] = columns[j] - factor * columns[j][k : k + 1, :]
        rows = rows - factor * rows[k : k + 1, :]
    return rows * lax.rsqrt(pivots)


def start_kernel(start_ref, out_ref):
    out_ref[...] = orth(orth(start_ref[...]))


def unpacked(tile, species):
    parts = [pltpu.roll(tile, (top - at) % LANES, 1) for top, at in triangle(species)]
    parts += [jnp.zeros((ROWS, LANES), jnp.float32)] * (LANES // ROWS - len(parts))
    upper = jnp.concatenate(parts, axis=0)
    row = lax.broadcasted_iota(jnp.int32, (LANES, LANES), 0)
    column = lax.broadcasted_iota(jnp.int32, (LANES, LANES), 1)
    gram = jnp.where(column >= row // ROWS * ROWS, upper, upper.T)
    return jnp.where((row < species) & (column < species), gram, 0.0)


def turn(rows, gram):
    return orth(orth(jnp.dot(rows, gram, precision=HIGH, preferred_element_type=jnp.float32)))


def doubled(rows, pitch):
    high, low = split(rows[:, :pitch])
    both = jnp.concatenate([high, low], axis=0)
    return jnp.concatenate([both, both], axis=1)


def projected(left, stack):
    both = dot32(left, stack, PLAIN)
    ranks = left.shape[0] // 2
    return both[:ranks] + both[ranks:]


def whole_call(kernel, out_shape, name, *args):
    return pl.pallas_call(
        kernel, out_shape=out_shape, compiler_params=SMALL, cost_estimate=lasting(0), name=name
    )(*args)


def basis_kernel(species, scale, tiles_ref, start_ref, rows_ref, basis_ref):
    gram = unpacked(jnp.sum(tiles_ref[...], axis=0) * scale, species)
    rows = start_ref[...]
    for _ in range(ITERS):
        rows = turn(rows, gram)
    rows_ref[...] = rows
    basis_ref[...] = rows[:, :species]


def basis_late_kernel(scale, top, cells_x, tiles_ref, start_ref, field_ref, *refs):
    rows_ref, basis_ref = refs[:2]
    late_refs, (buffer, core_ref, sem) = refs[2:-3], refs[-3:]
    species, _, cells = field_ref.shape
    pitch = up(species, HALF_ROWS)
    copy = pltpu.make_async_copy(field_ref.at[:, top:, :], buffer, sem)
    copy.start()
    gram = unpacked(jnp.sum(tiles_ref[...], axis=0) * scale, species)
    rows = start_ref[...]
    for _ in range(ITERS - 1):
        rows = turn(rows, gram)
    copy.wait()
    stack = stacked(buffer[...], pitch)
    rows = turn(rows, gram)
    rows_ref[...] = rows
    basis_ref[...] = rows[:, :species]
    core = projected(doubled(rows, pitch), stack)
    for i in range(core_ref.shape[0]):
        core_ref[i] = core[:, i * cells : (i + 1) * cells]
    for k, late_ref in zip(partners(len(late_refs)), late_refs, strict=True):
        for y in range(late_ref.shape[0]):
            late_ref[y] = core_ref[y * cells_x + partner(k)]


def basis_late(scale, early, count, tiles, first, field):
    species, cells_x, lines, cells = field.shape
    ranks = first.shape[0]
    late = lines - early
    return pl.pallas_call(
        functools.partial(basis_late_kernel, scale, early * cells_x, cells_x),
        in_specs=[VMEM, VMEM, ANY],
        out_specs=[VMEM] * (2 + count),
        out_shape=[
            jax.ShapeDtypeStruct((ranks, LANES), jnp.float32),
            jax.ShapeDtypeStruct((ranks, species), jnp.float32),
        ]
        + [jax.ShapeDtypeStruct((late, ranks, cells), jnp.float32)] * count,
        scratch_shapes=[
            pltpu.VMEM((species, late * cells_x, cells), jnp.float32),
            pltpu.VMEM((late * cells_x, ranks, cells), jnp.float32),
            pltpu.SemaphoreType.DMA,
        ],
        compiler_params=MIDDLE,
        cost_estimate=lasting(30),
        name="basis_late",
    )(tiles, first, by_rows(field))


def place(core, at, high_ref, low_ref):
    lines, ranks, cells = core.shape
    block = core.reshape(lines, ranks * cells)
    if lines % HALF_ROWS:
        fill = jnp.zeros((up(lines, HALF_ROWS) - lines, ranks * cells), jnp.float32)
        block = jnp.concatenate([block, fill], axis=0)
    high, low = split(block)
    high_ref[pl.ds(at, block.shape[0]), :] = high
    low_ref[pl.ds(at, block.shape[0]), :] = low


def ready_kernel(rows_ref, late_ref, *refs):
    pieces, (high_ref, low_ref, part_ref) = refs[:-3], refs[-3:]
    pitch = high_ref.shape[0] // len(pieces)
    species, early, cells = pieces[0].shape
    wide = up(species, HALF_ROWS)
    left = doubled(rows_ref[...], wide)
    for k, piece in zip(partners(len(pieces)), pieces, strict=True):
        core = projected(left, stacked(piece[...], wide))
        for y in range(early):
            part_ref[y] = core[:, y * cells : (y + 1) * cells]
        place(part_ref[...], pl.multiple_of(partner(k) * pitch, HALF_ROWS), high_ref, low_ref)
    at = pl.multiple_of(partner(0) * pitch + early, HALF_ROWS)
    place(late_ref[...], at, high_ref, low_ref)


def ready_rows(rows, own, pieces, lines):
    species, early, cells = pieces[0].shape
    ranks = rows.shape[0]
    shape = (len(pieces) * up(lines, HALF_ROWS), ranks * cells)
    return pl.pallas_call(
        ready_kernel,
        in_specs=[VMEM] * (2 + len(pieces)),
        out_specs=[VMEM, VMEM],
        out_shape=[jax.ShapeDtypeStruct(shape, jnp.bfloat16)] * 2,
        scratch_shapes=[pltpu.VMEM((early, ranks, cells), jnp.float32)],
        compiler_params=PARAMS,
        name="ready_rows",
    )(rows, own, *pieces)


def packing(lines, columns):
    groups = LANES // lines
    deep = -(-columns // groups)
    return groups, deep, up(deep, ROWS)


def line_kernel(axes, lines, early, count, *refs):
    n_gx, n_gy, n_sa = axes
    pieces, ready, (out_ref, high_ref, low_ref, gram_ref) = refs[:count], refs[count:-4], refs[-4:]
    pitch = high_ref.shape[0] // n_gy
    if ready:
        high_ref[...] = ready[0][...]
        low_ref[...] = ready[1][...]
    for k in range(count):
        block = partner(partners(n_gy)[n_gy - count + k])
        place(pieces[k][...], pl.multiple_of(block * pitch + early, HALF_ROWS), high_ref, low_ref)
    size = n_gy * pitch
    gram_ref[...] = jnp.zeros_like(gram_ref)
    gram_ref[:size, :size] = dot32(high_ref[...], low_ref[...], BY_LAST)
    cross = gram_ref[:size, :size]
    gram_ref[:size, :size] = dot32(high_ref[...], high_ref[...], BY_LAST) + cross + cross.T
    wide = gram_ref.shape[1]
    columns = lines * n_gy // (n_gx * n_sa)
    groups, deep, tall = packing(lines, columns)
    lane = lax.broadcasted_iota(jnp.int32, (tall, LANES), 1)
    for c in range(n_gx * n_sa):
        first = c * columns
        base = first // lines * pitch + first % lines
        bands = [gram_ref[base + g * deep : base + g * deep + tall, :] for g in range(groups)]
        for i in range(n_gy):
            tile = jnp.zeros((tall, LANES), jnp.float32)
            for g in range(groups):
                moved = pltpu.roll(bands[g], (g * lines - i * pitch) % wide, 1)[:, :LANES]
                tile = jnp.where((lane >= g * lines) & (lane < (g + 1) * lines), moved, tile)
            out_ref[((c // n_sa) * n_gy + i) * n_sa + c % n_sa] = tile


def line_tiles(pieces, ready, axes, lines, early):
    n_gx, n_gy, n_sa = axes
    _, ranks, cells = pieces[0].shape
    size = n_gy * up(lines, HALF_ROWS)
    _, _, tall = packing(lines, lines * n_gy // (n_gx * n_sa))
    return pl.pallas_call(
        functools.partial(line_kernel, axes, lines, early, len(pieces)),
        in_specs=[VMEM] * (len(pieces) + len(ready)),
        out_specs=VMEM,
        out_shape=jax.ShapeDtypeStruct((n_gx * n_gy * n_sa, tall, LANES), jnp.float32),
        scratch_shapes=[
            pltpu.VMEM((size, ranks * cells), jnp.bfloat16),
            pltpu.VMEM((size, ranks * cells), jnp.bfloat16),
            pltpu.VMEM((size + tall, up(size, LANES)), jnp.float32),
        ],
        compiler_params=PARAMS,
        name="line_tiles",
    )(*pieces, *ready)


def block_kernel(scale, tiles_ref, out_ref):
    columns, lines = out_ref.shape
    groups, deep, _ = packing(lines, columns)
    tile = jnp.sum(tiles_ref[...], axis=0) * scale
    for g in range(groups):
        part = tile if g == 0 else pltpu.roll(tile, LANES - g * lines, 1)
        high = min(deep, columns - g * deep)
        if high > 0:
            out_ref[g * deep : g * deep + high, :] = part[:high, :lines]


def partners(size):
    if size & (size - 1):
        raise ValueError("axis size")
    return sorted(range(size), key=lambda k: (k > 0, -k.bit_count(), k))


def exchanges(pieces, size):
    return pieces[:1] + [
        lax.ppermute(piece, "gy", [(a, a ^ k) for a in range(size)])
        for k, piece in zip(partners(size)[1:], pieces[1:], strict=True)
    ]


def on_device(field, start):
    species, cells_x, lines, cells_z = field.shape
    ranks = start.shape[1]
    n_gx, n_gy, n_sa = lax.axis_size("gx"), lax.axis_size("gy"), lax.axis_size("sa")
    axes, devices = (n_gx, n_gy, n_sa), n_gx * n_gy * n_sa
    total_x, total_y, total_z = cells_x * n_gx, lines * n_gy, cells_z * n_sa
    columns = total_y // (n_gx * n_sa)
    me = lax.axis_index("gy")
    parts_x = math.gcd(n_gy, cells_x)
    parts_z = n_gy // parts_x
    early = lines * 2 // 5 // HALF_ROWS * HALF_ROWS
    by_x = parts_x == cells_x and parts_z == 1 and early > 0
    early = early if by_x else 0

    tiles, *outgoing = gram_tiles(field, devices, early, n_gy if by_x else 0)
    tiles = lax.all_to_all(tiles, ALL, 0, 0, tiled=True)
    first = whole_call(
        start_kernel,
        jax.ShapeDtypeStruct((ranks, LANES), jnp.float32),
        "start_rows",
        jnp.pad(start.T, ((0, 0), (0, LANES - species))),
    )
    scale = 1.0 / (total_x * total_y * total_z)
    if by_x:
        received = exchanges(outgoing, n_gy)
        rows, basis, own, *pieces = basis_late(scale, early, n_gy, tiles, first, field)
        own, *pieces = exchanges([own, *pieces], n_gy)
        ready = ready_rows(rows, own, received, lines)
    else:
        rows, basis = whole_call(
            functools.partial(basis_kernel, species, scale),
            [
                jax.ShapeDtypeStruct((ranks, LANES), jnp.float32),
                jax.ShapeDtypeStruct((ranks, species), jnp.float32),
            ],
            "basis_rows",
            tiles,
            first,
        )
        wide_x, wide_z = cells_x // parts_x, cells_z // parts_z
        core = jnp.einsum("rs,sxyz->yrxz", rows[:, :species], field, precision=HIGH)
        pieces, ready = [], []
        for k in partners(n_gy):
            at = jnp.bitwise_xor(me, k)
            cut = lax.dynamic_slice(
                core,
                (0, 0, at // parts_z * wide_x, at % parts_z * wide_z),
                (lines, ranks, wide_x, wide_z),
            )
            pieces.append(cut.reshape(lines, -1, LANES))
        pieces = exchanges(pieces, n_gy)
    blocks = line_tiles(pieces, ready, axes, lines, early)
    blocks = lax.all_to_all(blocks, ALL, 0, 0, tiled=True)
    block = whole_call(
        functools.partial(block_kernel, 1.0 / (ranks * total_x * total_z)),
        jax.ShapeDtypeStruct((columns, lines), jnp.float32),
        "own_block",
        blocks,
    )
    return (basis.T, block.T)


def solution(mesh):
    in_specs = (P(None, "gx", "gy", "sa"), P())
    out_specs = (P(), P("gy", ("gx", "sa")))
    return jax.shard_map(
        on_device, mesh=mesh, in_specs=in_specs, out_specs=out_specs, check_vma=False
    )
```

```python
import functools
import math

import jax
import jax.numpy as jnp
from jax import lax
from jax.experimental import pallas as pl
from jax.experimental.pallas import tpu as pltpu
from jax.sharding import PartitionSpec as P

ITERS = 4
LANES = 128
ROWS = 8
HALF_ROWS = 16
HIGH = lax.Precision.HIGHEST
BY_LAST = (((1,), (1,)), ((), ()))
PLAIN = (((1,), (0,)), ((), ()))
ALL = ("gx", "gy", "sa")
VMEM = pl.BlockSpec(memory_space=pltpu.VMEM)
ANY = pl.BlockSpec(memory_space=pl.ANY)
SMALL = pltpu.CompilerParams(vmem_limit_bytes=4 * 2**20)
PARAMS = pltpu.CompilerParams(vmem_limit_bytes=16 * 2**20)
MIDDLE = pltpu.CompilerParams(vmem_limit_bytes=32 * 2**20)
LARGE = pltpu.CompilerParams(vmem_limit_bytes=61 * 2**20)


def lasting(time):
    return pl.CostEstimate(flops=0, bytes_accessed=int(time * 3.5e6), transcendentals=0)


def partner(k):
    return jnp.bitwise_xor(lax.axis_index("gy"), k)


def up(value, step):
    return -(-value // step) * step


def split(value):
    high = value.astype(jnp.bfloat16)
    low = (value - high.astype(jnp.float32)).astype(jnp.bfloat16)
    return high, low


def dot32(left, right, dims):
    return lax.dot_general(left, right, dims, preferred_element_type=jnp.float32)


def triangle(species):
    places, at = [], 0
    for top in range(0, species, ROWS):
        places.append((top, at))
        at += species - top
    return places


def stacked(rows, pitch):
    species, lines, cells = rows.shape
    high, low = split(rows.reshape(species, lines * cells))
    blank = jnp.zeros((pitch - species, lines * cells), jnp.bfloat16)
    return jnp.concatenate([high, blank, low, blank], axis=0)


def gram_kernel(cuts, cells_x, field_ref, tiles_ref, *refs):
    early_refs, (buffer, early, total, sems) = refs[:-4], refs[-4:]
    species = field_ref.shape[0]
    pitch = up(species, HALF_ROWS)
    spans = [slice(top, end) for top, end in zip(cuts[:-1], cuts[1:], strict=True)]
    copies = [
        pltpu.make_async_copy(field_ref.at[:, span, :], buffer.at[:, span, :], sems.at[i])
        for i, span in enumerate(spans)
    ]
    for copy in copies:
        copy.start()
    total[...] = jnp.zeros_like(total)
    sends = [
        pltpu.make_async_copy(early.at[k], ref, sems.at[len(copies) + k])
        for k, ref in enumerate(early_refs)
    ]
    for i, (copy, span) in enumerate(zip(copies, spans, strict=True)):
        copy.wait()
        for k, send in enumerate(sends if i == 0 else ()):
            early[k] = buffer[:, pl.ds(partner(partners(len(sends))[k]), early.shape[2], stride=cells_x), :]
            send.start()
        both = stacked(buffer[:, span, :], pitch)
        total[: 2 * pitch, : 2 * pitch] += dot32(both, both, BY_LAST)
    upper = total[:pitch, :] + total[pitch : 2 * pitch, :]
    upper = upper + pltpu.roll(upper, LANES - pitch, 1)
    lane = lax.broadcasted_iota(jnp.int32, (ROWS, LANES), 1)
    tile = jnp.zeros((ROWS, LANES), jnp.float32)
    for top, at in triangle(species):
        moved = pltpu.roll(upper[top : top + ROWS, :], (at - top) % LANES, 1)
        tile = jnp.where((lane >= at) & (lane < at + species - top), moved, tile)
    tiles_ref[...] = jnp.broadcast_to(tile[None], tiles_ref.shape)
    for send in sends:
        send.wait()


def by_rows(field):
    species, cells_x, lines, cells = field.shape
    return field.transpose(0, 2, 1, 3).reshape(species, lines * cells_x, cells)


def gram_tiles(field, devices, early, count):
    species, cells_x, lines, cells = field.shape
    rows = lines * cells_x
    pitch = up(species, HALF_ROWS)
    cuts = (0, max(up(rows * 2 // 5, ROWS), early * cells_x), up(rows * 3 // 4, ROWS), rows)
    return pl.pallas_call(
        functools.partial(gram_kernel, cuts, cells_x),
        in_specs=[ANY],
        out_specs=[VMEM] + [ANY] * count,
        out_shape=[jax.ShapeDtypeStruct((devices, ROWS, LANES), jnp.float32)]
        + [jax.ShapeDtypeStruct((species, early, cells), jnp.float32)] * count,
        scratch_shapes=[
            pltpu.VMEM((species, rows, cells), jnp.float32),
            pltpu.VMEM((max(count, 1), species, max(early, ROWS), cells), jnp.float32),
            pltpu.VMEM((up(2 * pitch, LANES), LANES), jnp.float32),
            pltpu.SemaphoreType.DMA((len(cuts) - 1 + count,)),
        ],
        compiler_params=LARGE,
        name="gram_tiles",
    )(by_rows(field))


def orth(rows):
    ranks = rows.shape[0]
    blocks = ranks // ROWS
    rows = [rows[b * ROWS : (b + 1) * ROWS] for b in range(blocks)]
    shape = rows[0].shape
    index = lax.broadcasted_iota(jnp.int32, shape, 0)
    columns, pivots = [], []
    for k in range(ranks):
        row = rows[k // ROWS][k % ROWS : k % ROWS + 1, :]
        columns.append(
            {
                b: jnp.broadcast_to(jnp.sum(rows[b] * row, axis=1, keepdims=True), shape)
                for b in range(k // ROWS, blocks)
            }
        )
    for k in range(ranks):
        own, at = divmod(k, ROWS)
        pivot = columns[k][own][at : at + 1, :]
        below = {**columns[k], own: jnp.where(index > at, columns[k][own], 0.0)}
        inverse = 1.0 / pivot
        factor = {b: part * inverse for b, part in below.items()}
        if at == 0:
            pivots.append(jnp.broadcast_to(pivot, shape))
        pivots[own] = jnp.where(index == at, pivot, pivots[own])
        for j in range(k + 1, ranks):
            entry = columns[k][j // ROWS][j % ROWS : j % ROWS + 1, :]
            for b in columns[j]:
                columns[j][b] = columns[j][b] - factor[b] * entry
        row = rows[own][at : at + 1, :]
        for b in factor:
            rows[b] = rows[b] - factor[b] * row
    return jnp.concatenate([r * lax.rsqrt(p) for r, p in zip(rows, pivots, strict=True)], axis=0)


def start_kernel(start_ref, out_ref):
    out_ref[...] = orth(orth(start_ref[...]))


def unpacked(tile, species):
    parts = [pltpu.roll(tile, (top - at) % LANES, 1) for top, at in triangle(species)]
    parts += [jnp.zeros((ROWS, LANES), jnp.float32)] * (LANES // ROWS - len(parts))
    upper = jnp.concatenate(parts, axis=0)
    row = lax.broadcasted_iota(jnp.int32, (LANES, LANES), 0)
    column = lax.broadcasted_iota(jnp.int32, (LANES, LANES), 1)
    gram = jnp.where(column >= row // ROWS * ROWS, upper, upper.T)
    return jnp.where((row < species) & (column < species), gram, 0.0)


def turn(rows, gram):
    return orth(orth(jnp.dot(rows, gram, precision=HIGH, preferred_element_type=jnp.float32)))


def doubled(rows, pitch):
    high, low = split(rows[:, :pitch])
    both = jnp.concatenate([high, low], axis=0)
    return jnp.concatenate([both, both], axis=1)


def projected(left, stack):
    both = dot32(left, stack, PLAIN)
    ranks = left.shape[0] // 2
    return both[:ranks] + both[ranks:]


def whole_call(kernel, out_shape, name, *args):
    return pl.pallas_call(
        kernel, out_shape=out_shape, compiler_params=SMALL, cost_estimate=lasting(0), name=name
    )(*args)


def basis_kernel(species, scale, tiles_ref, start_ref, rows_ref, basis_ref):
    gram = unpacked(jnp.sum(tiles_ref[...], axis=0) * scale, species)
    rows = start_ref[...]
    for _ in range(ITERS):
        rows = turn(rows, gram)
    rows_ref[...] = rows
    basis_ref[...] = rows[:, :species]


def basis_late_kernel(scale, top, cells_x, tiles_ref, start_ref, field_ref, *refs):
    rows_ref, basis_ref = refs[:2]
    late_refs, (buffer, core_ref, sem) = refs[2:-3], refs[-3:]
    species, _, cells = field_ref.shape
    pitch = up(species, HALF_ROWS)
    copy = pltpu.make_async_copy(field_ref.at[:, top:, :], buffer, sem)
    copy.start()
    gram = unpacked(jnp.sum(tiles_ref[...], axis=0) * scale, species)
    rows = start_ref[...]
    for _ in range(ITERS - 1):
        rows = turn(rows, gram)
    copy.wait()
    stack = stacked(buffer[...], pitch)
    rows = turn(rows, gram)
    rows_ref[...] = rows
    basis_ref[...] = rows[:, :species]
    core = projected(doubled(rows, pitch), stack)
    for i in range(core_ref.shape[0]):
        core_ref[i] = core[:, i * cells : (i + 1) * cells]
    for k, late_ref in zip(partners(len(late_refs)), late_refs, strict=True):
        for y in range(late_ref.shape[0]):
            late_ref[y] = core_ref[y * cells_x + partner(k)]


def basis_late(scale, early, count, tiles, first, field):
    species, cells_x, lines, cells = field.shape
    ranks = first.shape[0]
    late = lines - early
    return pl.pallas_call(
        functools.partial(basis_late_kernel, scale, early * cells_x, cells_x),
        in_specs=[VMEM, VMEM, ANY],
        out_specs=[VMEM] * (2 + count),
        out_shape=[
            jax.ShapeDtypeStruct((ranks, LANES), jnp.float32),
            jax.ShapeDtypeStruct((ranks, species), jnp.float32),
        ]
        + [jax.ShapeDtypeStruct((late, ranks, cells), jnp.float32)] * count,
        scratch_shapes=[
            pltpu.VMEM((species, late * cells_x, cells), jnp.float32),
            pltpu.VMEM((late * cells_x, ranks, cells), jnp.float32),
            pltpu.SemaphoreType.DMA,
        ],
        compiler_params=MIDDLE,
        cost_estimate=lasting(30),
        name="basis_late",
    )(tiles, first, by_rows(field))


def place(core, at, high_ref, low_ref):
    lines, ranks, cells = core.shape
    block = core.reshape(lines, ranks * cells)
    if lines % HALF_ROWS:
        fill = jnp.zeros((up(lines, HALF_ROWS) - lines, ranks * cells), jnp.float32)
        block = jnp.concatenate([block, fill], axis=0)
    high, low = split(block)
    high_ref[pl.ds(at, block.shape[0]), :] = high
    low_ref[pl.ds(at, block.shape[0]), :] = low


def ready_kernel(rows_ref, late_ref, *refs):
    pieces, (high_ref, low_ref, part_ref) = refs[:-3], refs[-3:]
    pitch = high_ref.shape[0] // len(pieces)
    species, early, cells = pieces[0].shape
    wide = up(species, HALF_ROWS)
    left = doubled(rows_ref[...], wide)
    for k, piece in zip(partners(len(pieces)), pieces, strict=True):
        core = projected(left, stacked(piece[...], wide))
        for y in range(early):
            part_ref[y] = core[:, y * cells : (y + 1) * cells]
        place(part_ref[...], pl.multiple_of(partner(k) * pitch, HALF_ROWS), high_ref, low_ref)
    at = pl.multiple_of(partner(0) * pitch + early, HALF_ROWS)
    place(late_ref[...], at, high_ref, low_ref)


def ready_rows(rows, own, pieces, lines):
    species, early, cells = pieces[0].shape
    ranks = rows.shape[0]
    shape = (len(pieces) * up(lines, HALF_ROWS), ranks * cells)
    return pl.pallas_call(
        ready_kernel,
        in_specs=[VMEM] * (2 + len(pieces)),
        out_specs=[VMEM, VMEM],
        out_shape=[jax.ShapeDtypeStruct(shape, jnp.bfloat16)] * 2,
        scratch_shapes=[pltpu.VMEM((early, ranks, cells), jnp.float32)],
        compiler_params=PARAMS,
        name="ready_rows",
    )(rows, own, *pieces)


def packing(lines, columns):
    groups = LANES // lines
    deep = -(-columns // groups)
    return groups, deep, up(deep, ROWS)


def line_kernel(axes, lines, early, count, *refs):
    n_gx, n_gy, n_sa = axes
    pieces, ready, (out_ref, high_ref, low_ref, gram_ref) = refs[:count], refs[count:-4], refs[-4:]
    pitch = high_ref.shape[0] // n_gy
    if ready:
        high_ref[...] = ready[0][...]
        low_ref[...] = ready[1][...]
    for k in range(count):
        block = partner(partners(n_gy)[n_gy - count + k])
        place(pieces[k][...], pl.multiple_of(block * pitch + early, HALF_ROWS), high_ref, low_ref)
    size = n_gy * pitch
    gram_ref[...] = jnp.zeros_like(gram_ref)
    gram_ref[:size, :size] = dot32(high_ref[...], low_ref[...], BY_LAST)
    cross = gram_ref[:size, :size]
    gram_ref[:size, :size] = dot32(high_ref[...], high_ref[...], BY_LAST) + cross + cross.T
    wide = gram_ref.shape[1]
    columns = lines * n_gy // (n_gx * n_sa)
    groups, deep, tall = packing(lines, columns)
    lane = lax.broadcasted_iota(jnp.int32, (tall, LANES), 1)
    for c in range(n_gx * n_sa):
        first = c * columns
        base = first // lines * pitch + first % lines
        bands = [gram_ref[base + g * deep : base + g * deep + tall, :] for g in range(groups)]
        for i in range(n_gy):
            tile = jnp.zeros((tall, LANES), jnp.float32)
            for g in range(groups):
                moved = pltpu.roll(bands[g], (g * lines - i * pitch) % wide, 1)[:, :LANES]
                tile = jnp.where((lane >= g * lines) & (lane < (g + 1) * lines), moved, tile)
            out_ref[((c // n_sa) * n_gy + i) * n_sa + c % n_sa] = tile


def line_tiles(pieces, ready, axes, lines, early):
    n_gx, n_gy, n_sa = axes
    _, ranks, cells = pieces[0].shape
    size = n_gy * up(lines, HALF_ROWS)
    _, _, tall = packing(lines, lines * n_gy // (n_gx * n_sa))
    return pl.pallas_call(
        functools.partial(line_kernel, axes, lines, early, len(pieces)),
        in_specs=[VMEM] * (len(pieces) + len(ready)),
        out_specs=VMEM,
        out_shape=jax.ShapeDtypeStruct((n_gx * n_gy * n_sa, tall, LANES), jnp.float32),
        scratch_shapes=[
            pltpu.VMEM((size, ranks * cells), jnp.bfloat16),
            pltpu.VMEM((size, ranks * cells), jnp.bfloat16),
            pltpu.VMEM((size + tall, up(size, LANES)), jnp.float32),
        ],
        compiler_params=PARAMS,
        name="line_tiles",
    )(*pieces, *ready)


def block_kernel(scale, tiles_ref, out_ref):
    columns, lines = out_ref.shape
    groups, deep, _ = packing(lines, columns)
    tile = jnp.sum(tiles_ref[...], axis=0) * scale
    for g in range(groups):
        part = tile if g == 0 else pltpu.roll(tile, LANES - g * lines, 1)
        high = min(deep, columns - g * deep)
        if high > 0:
            out_ref[g * deep : g * deep + high, :] = part[:high, :lines]


def partners(size):
    if size & (size - 1):
        raise ValueError("axis size")
    return sorted(range(size), key=lambda k: (k > 0, -k.bit_count(), k))


def exchanges(pieces, size):
    return pieces[:1] + [
        lax.ppermute(piece, "gy", [(a, a ^ k) for a in range(size)])
        for k, piece in zip(partners(size)[1:], pieces[1:], strict=True)
    ]


def on_device(field, start):
    species, cells_x, lines, cells_z = field.shape
    ranks = start.shape[1]
    n_gx, n_gy, n_sa = lax.axis_size("gx"), lax.axis_size("gy"), lax.axis_size("sa")
    axes, devices = (n_gx, n_gy, n_sa), n_gx * n_gy * n_sa
    total_x, total_y, total_z = cells_x * n_gx, lines * n_gy, cells_z * n_sa
    columns = total_y // (n_gx * n_sa)
    me = lax.axis_index("gy")
    parts_x = math.gcd(n_gy, cells_x)
    parts_z = n_gy // parts_x
    early = lines * 2 // 5 // HALF_ROWS * HALF_ROWS
    by_x = parts_x == cells_x and parts_z == 1 and early > 0
    early = early if by_x else 0

    tiles, *outgoing = gram_tiles(field, devices, early, n_gy if by_x else 0)
    tiles = lax.all_to_all(tiles, ALL, 0, 0, tiled=True)
    first = whole_call(
        start_kernel,
        jax.ShapeDtypeStruct((ranks, LANES), jnp.float32),
        "start_rows",
        jnp.pad(start.T, ((0, 0), (0, LANES - species))),
    )
    scale = 1.0 / (total_x * total_y * total_z)
    if by_x:
        received = exchanges(outgoing, n_gy)
        rows, basis, own, *pieces = basis_late(scale, early, n_gy, tiles, first, field)
        own, *pieces = exchanges([own, *pieces], n_gy)
        ready = ready_rows(rows, own, received, lines)
    else:
        rows, basis = whole_call(
            functools.partial(basis_kernel, species, scale),
            [
                jax.ShapeDtypeStruct((ranks, LANES), jnp.float32),
                jax.ShapeDtypeStruct((ranks, species), jnp.float32),
            ],
            "basis_rows",
            tiles,
            first,
        )
        wide_x, wide_z = cells_x // parts_x, cells_z // parts_z
        core = jnp.einsum("rs,sxyz->yrxz", rows[:, :species], field, precision=HIGH)
        pieces, ready = [], []
        for k in partners(n_gy):
            at = jnp.bitwise_xor(me, k)
            cut = lax.dynamic_slice(
                core,
                (0, 0, at // parts_z * wide_x, at % parts_z * wide_z),
                (lines, ranks, wide_x, wide_z),
            )
            pieces.append(cut.reshape(lines, -1, LANES))
        pieces = exchanges(pieces, n_gy)
    blocks = line_tiles(pieces, ready, axes, lines, early)
    blocks = lax.all_to_all(blocks, ALL, 0, 0, tiled=True)
    block = whole_call(
        functools.partial(block_kernel, 1.0 / (ranks * total_x * total_z)),
        jax.ShapeDtypeStruct((columns, lines), jnp.float32),
        "own_block",
        blocks,
    )
    return (basis.T, block.T)


def solution(mesh):
    in_specs = (P(None, "gx", "gy", "sa"), P())
    out_specs = (P(), P("gy", ("gx", "sa")))
    return jax.shard_map(
        on_device, mesh=mesh, in_specs=in_specs, out_specs=out_specs, check_vma=False
    )
```

```python
import functools
import math

import jax
import jax.numpy as jnp
from jax import lax
from jax.experimental import pallas as pl
from jax.experimental.pallas import tpu as pltpu
from jax.sharding import PartitionSpec as P

ITERS = 4
LANES = 128
ROWS = 8
HALF_ROWS = 16
HIGH = lax.Precision.HIGHEST
BY_LAST = (((1,), (1,)), ((), ()))
PLAIN = (((1,), (0,)), ((), ()))
ALL = ("gx", "gy", "sa")
VMEM = pl.BlockSpec(memory_space=pltpu.VMEM)
ANY = pl.BlockSpec(memory_space=pl.ANY)
SMALL = pltpu.CompilerParams(vmem_limit_bytes=4 * 2**20)
PARAMS = pltpu.CompilerParams(vmem_limit_bytes=16 * 2**20)
MIDDLE = pltpu.CompilerParams(vmem_limit_bytes=32 * 2**20)
LARGE = pltpu.CompilerParams(vmem_limit_bytes=61 * 2**20)


def lasting(time):
    return pl.CostEstimate(flops=0, bytes_accessed=int(time * 3.5e6), transcendentals=0)


def partner(k):
    return jnp.bitwise_xor(lax.axis_index("gy"), k)


def up(value, step):
    return -(-value // step) * step


def split(value):
    high = value.astype(jnp.bfloat16)
    low = (value - high.astype(jnp.float32)).astype(jnp.bfloat16)
    return high, low


def dot32(left, right, dims):
    return lax.dot_general(left, right, dims, preferred_element_type=jnp.float32)


def triangle(species):
    places, at = [], 0
    for top in range(0, species, ROWS):
        places.append((top, at))
        at += species - top
    return places


def stacked(rows, pitch):
    species, lines, cells = rows.shape
    high, low = split(rows.reshape(species, lines * cells))
    blank = jnp.zeros((pitch - species, lines * cells), jnp.bfloat16)
    return jnp.concatenate([high, blank, low, blank], axis=0)


def gram_kernel(cuts, cells_x, field_ref, tiles_ref, *refs):
    early_refs, (buffer, early, total, sems) = refs[:-4], refs[-4:]
    species = field_ref.shape[0]
    pitch = up(species, HALF_ROWS)
    spans = [slice(top, end) for top, end in zip(cuts[:-1], cuts[1:], strict=True)]
    copies = [
        pltpu.make_async_copy(field_ref.at[:, span, :], buffer.at[:, span, :], sems.at[i])
        for i, span in enumerate(spans)
    ]
    for copy in copies:
        copy.start()
    total[...] = jnp.zeros_like(total)
    sends = [
        pltpu.make_async_copy(early.at[k], ref, sems.at[len(copies) + k])
        for k, ref in enumerate(early_refs)
    ]
    for i, (copy, span) in enumerate(zip(copies, spans, strict=True)):
        copy.wait()
        for k, send in enumerate(sends if i == 0 else ()):
            early[k] = buffer[:, pl.ds(partner(partners(len(sends))[k]), early.shape[2], stride=cells_x), :]
            send.start()
        both = stacked(buffer[:, span, :], pitch)
        total[: 2 * pitch, : 2 * pitch] += dot32(both, both, BY_LAST)
    upper = total[:pitch, :] + total[pitch : 2 * pitch, :]
    upper = upper + pltpu.roll(upper, LANES - pitch, 1)
    lane = lax.broadcasted_iota(jnp.int32, (ROWS, LANES), 1)
    tile = jnp.zeros((ROWS, LANES), jnp.float32)
    for top, at in triangle(species):
        moved = pltpu.roll(upper[top : top + ROWS, :], (at - top) % LANES, 1)
        tile = jnp.where((lane >= at) & (lane < at + species - top), moved, tile)
    tiles_ref[...] = jnp.broadcast_to(tile[None], tiles_ref.shape)
    for send in sends:
        send.wait()


def by_rows(field):
    species, cells_x, lines, cells = field.shape
    return field.transpose(0, 2, 1, 3).reshape(species, lines * cells_x, cells)


def gram_tiles(field, devices, early, count):
    species, cells_x, lines, cells = field.shape
    rows = lines * cells_x
    pitch = up(species, HALF_ROWS)
    cuts = (0, max(up(rows * 2 // 5, ROWS), early * cells_x), up(rows * 3 // 4, ROWS), rows)
    return pl.pallas_call(
        functools.partial(gram_kernel, cuts, cells_x),
        in_specs=[ANY],
        out_specs=[VMEM] + [ANY] * count,
        out_shape=[jax.ShapeDtypeStruct((devices, ROWS, LANES), jnp.float32)]
        + [jax.ShapeDtypeStruct((species, early, cells), jnp.float32)] * count,
        scratch_shapes=[
            pltpu.VMEM((species, rows, cells), jnp.float32),
            pltpu.VMEM((max(count, 1), species, max(early, ROWS), cells), jnp.float32),
            pltpu.VMEM((up(2 * pitch, LANES), LANES), jnp.float32),
            pltpu.SemaphoreType.DMA((len(cuts) - 1 + count,)),
        ],
        compiler_params=LARGE,
        name="gram_tiles",
    )(by_rows(field))


def orth(rows):
    ranks = rows.shape[0]
    blocks = ranks // ROWS
    rows = [rows[b * ROWS : (b + 1) * ROWS] for b in range(blocks)]
    shape = rows[0].shape
    index = lax.broadcasted_iota(jnp.int32, shape, 0)
    columns, pivots = [], []
    for k in range(ranks):
        row = rows[k // ROWS][k % ROWS : k % ROWS + 1, :]
        columns.append(
            {
                b: jnp.broadcast_to(jnp.sum(rows[b] * row, axis=1, keepdims=True), shape)
                for b in range(k // ROWS, blocks)
            }
        )
    for k in range(ranks):
        own, at = divmod(k, ROWS)
        pivot = columns[k][own][at : at + 1, :]
        below = {**columns[k], own: jnp.where(index > at, columns[k][own], 0.0)}
        inverse = 1.0 / pivot
        factor = {b: part * inverse for b, part in below.items()}
        if at == 0:
            pivots.append(jnp.broadcast_to(pivot, shape))
        pivots[own] = jnp.where(index == at, pivot, pivots[own])
        for j in range(k + 1, ranks):
            entry = columns[k][j // ROWS][j % ROWS : j % ROWS + 1, :]
            for b in columns[j]:
                columns[j][b] = columns[j][b] - factor[b] * entry
        row = rows[own][at : at + 1, :]
        for b in factor:
            rows[b] = rows[b] - factor[b] * row
    return jnp.concatenate([r * lax.rsqrt(p) for r, p in zip(rows, pivots, strict=True)], axis=0)


def start_kernel(start_ref, out_ref):
    out_ref[...] = orth(orth(start_ref[...]))


def unpacked(tile, species):
    parts = [pltpu.roll(tile, (top - at) % LANES, 1) for top, at in triangle(species)]
    parts += [jnp.zeros((ROWS, LANES), jnp.float32)] * (LANES // ROWS - len(parts))
    upper = jnp.concatenate(parts, axis=0)
    row = lax.broadcasted_iota(jnp.int32, (LANES, LANES), 0)
    column = lax.broadcasted_iota(jnp.int32, (LANES, LANES), 1)
    gram = jnp.where(column >= row // ROWS * ROWS, upper, upper.T)
    return jnp.where((row < species) & (column < species), gram, 0.0)


def turn(rows, gram):
    return orth(orth(jnp.dot(rows, gram, precision=HIGH, preferred_element_type=jnp.float32)))


def doubled(rows, pitch):
    high, low = split(rows[:, :pitch])
    both = jnp.concatenate([high, low], axis=0)
    return jnp.concatenate([both, both], axis=1)


def projected(left, stack):
    both = dot32(left, stack, PLAIN)
    ranks = left.shape[0] // 2
    return both[:ranks] + both[ranks:]


def whole_call(kernel, out_shape, name, *args):
    return pl.pallas_call(
        kernel, out_shape=out_shape, compiler_params=SMALL, cost_estimate=lasting(0), name=name
    )(*args)


def basis_kernel(species, scale, tiles_ref, start_ref, rows_ref, basis_ref):
    gram = unpacked(jnp.sum(tiles_ref[...], axis=0) * scale, species)
    rows = start_ref[...]
    for _ in range(ITERS):
        rows = turn(rows, gram)
    rows_ref[...] = rows
    basis_ref[...] = rows[:, :species]


def basis_late_kernel(scale, top, cells_x, tiles_ref, start_ref, field_ref, *refs):
    rows_ref, basis_ref = refs[:2]
    late_refs, (buffer, core_ref, sem) = refs[2:-3], refs[-3:]
    species, _, cells = field_ref.shape
    pitch = up(species, HALF_ROWS)
    copy = pltpu.make_async_copy(field_ref.at[:, top:, :], buffer, sem)
    copy.start()
    gram = unpacked(jnp.sum(tiles_ref[...], axis=0) * scale, species)
    rows = start_ref[...]
    for _ in range(ITERS - 1):
        rows = turn(rows, gram)
    copy.wait()
    stack = stacked(buffer[...], pitch)
    rows = turn(rows, gram)
    rows_ref[...] = rows
    basis_ref[...] = rows[:, :species]
    core = projected(doubled(rows, pitch), stack)
    for i in range(core_ref.shape[0]):
        core_ref[i] = core[:, i * cells : (i + 1) * cells]
    for k, late_ref in zip(partners(len(late_refs)), late_refs, strict=True):
        for y in range(late_ref.shape[0]):
            late_ref[y] = core_ref[y * cells_x + partner(k)]


def basis_late(scale, early, count, tiles, first, field):
    species, cells_x, lines, cells = field.shape
    ranks = first.shape[0]
    late = lines - early
    return pl.pallas_call(
        functools.partial(basis_late_kernel, scale, early * cells_x, cells_x),
        in_specs=[VMEM, VMEM, ANY],
        out_specs=[VMEM] * (2 + count),
        out_shape=[
            jax.ShapeDtypeStruct((ranks, LANES), jnp.float32),
            jax.ShapeDtypeStruct((ranks, species), jnp.float32),
        ]
        + [jax.ShapeDtypeStruct((late, ranks, cells), jnp.float32)] * count,
        scratch_shapes=[
            pltpu.VMEM((species, late * cells_x, cells), jnp.float32),
            pltpu.VMEM((late * cells_x, ranks, cells), jnp.float32),
            pltpu.SemaphoreType.DMA,
        ],
        compiler_params=MIDDLE,
        cost_estimate=lasting(30),
        name="basis_late",
    )(tiles, first, by_rows(field))


def place(core, at, high_ref, low_ref):
    lines, ranks, cells = core.shape
    block = core.reshape(lines, ranks * cells)
    if lines % HALF_ROWS:
        fill = jnp.zeros((up(lines, HALF_ROWS) - lines, ranks * cells), jnp.float32)
        block = jnp.concatenate([block, fill], axis=0)
    high, low = split(block)
    high_ref[pl.ds(at, block.shape[0]), :] = high
    low_ref[pl.ds(at, block.shape[0]), :] = low


def ready_kernel(rows_ref, late_ref, *refs):
    pieces, (high_ref, low_ref, part_ref) = refs[:-3], refs[-3:]
    pitch = high_ref.shape[0] // len(pieces)
    species, early, cells = pieces[0].shape
    wide = up(species, HALF_ROWS)
    left = doubled(rows_ref[...], wide)
    for k, piece in zip(partners(len(pieces)), pieces, strict=True):
        core = projected(left, stacked(piece[...], wide))
        for y in range(early):
            part_ref[y] = core[:, y * cells : (y + 1) * cells]
        place(part_ref[...], pl.multiple_of(partner(k) * pitch, HALF_ROWS), high_ref, low_ref)
    at = pl.multiple_of(partner(0) * pitch + early, HALF_ROWS)
    place(late_ref[...], at, high_ref, low_ref)


def ready_rows(rows, own, pieces, lines):
    species, early, cells = pieces[0].shape
    ranks = rows.shape[0]
    shape = (len(pieces) * up(lines, HALF_ROWS), ranks * cells)
    return pl.pallas_call(
        ready_kernel,
        in_specs=[VMEM] * (2 + len(pieces)),
        out_specs=[VMEM, VMEM],
        out_shape=[jax.ShapeDtypeStruct(shape, jnp.bfloat16)] * 2,
        scratch_shapes=[pltpu.VMEM((early, ranks, cells), jnp.float32)],
        compiler_params=PARAMS,
        name="ready_rows",
    )(rows, own, *pieces)


def packing(lines, columns):
    groups = LANES // lines
    deep = -(-columns // groups)
    return groups, deep, up(deep, ROWS)


def line_kernel(axes, lines, early, count, *refs):
    n_gx, n_gy, n_sa = axes
    pieces, ready, (out_ref, high_ref, low_ref, gram_ref) = refs[:count], refs[count:-4], refs[-4:]
    pitch = high_ref.shape[0] // n_gy
    if ready:
        high_ref[...] = ready[0][...]
        low_ref[...] = ready[1][...]
    for k in range(count):
        block = partner(partners(n_gy)[n_gy - count + k])
        place(pieces[k][...], pl.multiple_of(block * pitch + early, HALF_ROWS), high_ref, low_ref)
    size = n_gy * pitch
    gram_ref[...] = jnp.zeros_like(gram_ref)
    gram_ref[:size, :size] = dot32(high_ref[...], low_ref[...], BY_LAST)
    cross = gram_ref[:size, :size]
    gram_ref[:size, :size] = dot32(high_ref[...], high_ref[...], BY_LAST) + cross + cross.T
    wide = gram_ref.shape[1]
    columns = lines * n_gy // (n_gx * n_sa)
    groups, deep, tall = packing(lines, columns)
    lane = lax.broadcasted_iota(jnp.int32, (tall, LANES), 1)
    for c in range(n_gx * n_sa):
        first = c * columns
        base = first // lines * pitch + first % lines
        bands = [gram_ref[base + g * deep : base + g * deep + tall, :] for g in range(groups)]
        for i in range(n_gy):
            tile = jnp.zeros((tall, LANES), jnp.float32)
            for g in range(groups):
                moved = pltpu.roll(bands[g], (g * lines - i * pitch) % wide, 1)[:, :LANES]
                tile = jnp.where((lane >= g * lines) & (lane < (g + 1) * lines), moved, tile)
            out_ref[((c // n_sa) * n_gy + i) * n_sa + c % n_sa] = tile


def line_tiles(pieces, ready, axes, lines, early):
    n_gx, n_gy, n_sa = axes
    _, ranks, cells = pieces[0].shape
    size = n_gy * up(lines, HALF_ROWS)
    _, _, tall = packing(lines, lines * n_gy // (n_gx * n_sa))
    return pl.pallas_call(
        functools.partial(line_kernel, axes, lines, early, len(pieces)),
        in_specs=[VMEM] * (len(pieces) + len(ready)),
        out_specs=VMEM,
        out_shape=jax.ShapeDtypeStruct((n_gx * n_gy * n_sa, tall, LANES), jnp.float32),
        scratch_shapes=[
            pltpu.VMEM((size, ranks * cells), jnp.bfloat16),
            pltpu.VMEM((size, ranks * cells), jnp.bfloat16),
            pltpu.VMEM((size + tall, up(size, LANES)), jnp.float32),
        ],
        compiler_params=PARAMS,
        name="line_tiles",
    )(*pieces, *ready)


def block_kernel(scale, tiles_ref, out_ref):
    columns, lines = out_ref.shape
    groups, deep, _ = packing(lines, columns)
    tile = jnp.sum(tiles_ref[...], axis=0) * scale
    for g in range(groups):
        part = tile if g == 0 else pltpu.roll(tile, LANES - g * lines, 1)
        high = min(deep, columns - g * deep)
        if high > 0:
            out_ref[g * deep : g * deep + high, :] = part[:high, :lines]


def partners(size):
    if size & (size - 1):
        raise ValueError("axis size")
    return sorted(range(size), key=lambda k: (k > 0, -k.bit_count(), -k))


def exchanges(pieces, size):
    return pieces[:1] + [
        lax.ppermute(piece, "gy", [(a, a ^ k) for a in range(size)])
        for k, piece in zip(partners(size)[1:], pieces[1:], strict=True)
    ]


def on_device(field, start):
    species, cells_x, lines, cells_z = field.shape
    ranks = start.shape[1]
    n_gx, n_gy, n_sa = lax.axis_size("gx"), lax.axis_size("gy"), lax.axis_size("sa")
    axes, devices = (n_gx, n_gy, n_sa), n_gx * n_gy * n_sa
    total_x, total_y, total_z = cells_x * n_gx, lines * n_gy, cells_z * n_sa
    columns = total_y // (n_gx * n_sa)
    me = lax.axis_index("gy")
    parts_x = math.gcd(n_gy, cells_x)
    parts_z = n_gy // parts_x
    early = lines * 2 // 5 // HALF_ROWS * HALF_ROWS
    by_x = parts_x == cells_x and parts_z == 1 and early > 0
    early = early if by_x else 0

    tiles, *outgoing = gram_tiles(field, devices, early, n_gy if by_x else 0)
    tiles = lax.all_to_all(tiles, ALL, 0, 0, tiled=True)
    first = whole_call(
        start_kernel,
        jax.ShapeDtypeStruct((ranks, LANES), jnp.float32),
        "start_rows",
        jnp.pad(start.T, ((0, 0), (0, LANES - species))),
    )
    scale = 1.0 / (total_x * total_y * total_z)
    if by_x:
        received = exchanges(outgoing, n_gy)
        rows, basis, own, *pieces = basis_late(scale, early, n_gy, tiles, first, field)
        own, *pieces = exchanges([own, *pieces], n_gy)
        ready = ready_rows(rows, own, received, lines)
    else:
        rows, basis = whole_call(
            functools.partial(basis_kernel, species, scale),
            [
                jax.ShapeDtypeStruct((ranks, LANES), jnp.float32),
                jax.ShapeDtypeStruct((ranks, species), jnp.float32),
            ],
            "basis_rows",
            tiles,
            first,
        )
        wide_x, wide_z = cells_x // parts_x, cells_z // parts_z
        core = jnp.einsum("rs,sxyz->yrxz", rows[:, :species], field, precision=HIGH)
        pieces, ready = [], []
        for k in partners(n_gy):
            at = jnp.bitwise_xor(me, k)
            cut = lax.dynamic_slice(
                core,
                (0, 0, at // parts_z * wide_x, at % parts_z * wide_z),
                (lines, ranks, wide_x, wide_z),
            )
            pieces.append(cut.reshape(lines, -1, LANES))
        pieces = exchanges(pieces, n_gy)
    blocks = line_tiles(pieces, ready, axes, lines, early)
    blocks = lax.all_to_all(blocks, ALL, 0, 0, tiled=True)
    block = whole_call(
        functools.partial(block_kernel, 1.0 / (ranks * total_x * total_z)),
        jax.ShapeDtypeStruct((columns, lines), jnp.float32),
        "own_block",
        blocks,
    )
    return (basis.T, block.T)


def solution(mesh):
    in_specs = (P(None, "gx", "gy", "sa"), P())
    out_specs = (P(), P("gy", ("gx", "sa")))
    return jax.shard_map(
        on_device, mesh=mesh, in_specs=in_specs, out_specs=out_specs, check_vma=False
    )
```

```python
import functools
import math

import jax
import jax.numpy as jnp
from jax import lax
from jax.experimental import pallas as pl
from jax.experimental.pallas import tpu as pltpu
from jax.sharding import PartitionSpec as P

ITERS = 4
LANES = 128
ROWS = 8
HALF_ROWS = 16
HIGH = lax.Precision.HIGHEST
BY_LAST = (((1,), (1,)), ((), ()))
PLAIN = (((1,), (0,)), ((), ()))
ALL = ("gx", "gy", "sa")
VMEM = pl.BlockSpec(memory_space=pltpu.VMEM)
ANY = pl.BlockSpec(memory_space=pl.ANY)
SMALL = pltpu.CompilerParams(vmem_limit_bytes=4 * 2**20)
PARAMS = pltpu.CompilerParams(vmem_limit_bytes=16 * 2**20)
MIDDLE = pltpu.CompilerParams(vmem_limit_bytes=32 * 2**20)
LARGE = pltpu.CompilerParams(vmem_limit_bytes=61 * 2**20)


def lasting(time):
    return pl.CostEstimate(flops=0, bytes_accessed=int(time * 3.5e6), transcendentals=0)


def partner(k):
    return jnp.bitwise_xor(lax.axis_index("gy"), k)


def up(value, step):
    return -(-value // step) * step


def split(value):
    high = value.astype(jnp.bfloat16)
    low = (value - high.astype(jnp.float32)).astype(jnp.bfloat16)
    return high, low


def dot32(left, right, dims):
    return lax.dot_general(left, right, dims, preferred_element_type=jnp.float32)


def triangle(species):
    places, at = [], 0
    for top in range(0, species, ROWS):
        places.append((top, at))
        at += species - top
    return places


def stacked(rows, pitch):
    species, lines, cells = rows.shape
    high, low = split(rows.reshape(species, lines * cells))
    blank = jnp.zeros((pitch - species, lines * cells), jnp.bfloat16)
    return jnp.concatenate([high, blank, low, blank], axis=0)


def gram_kernel(cuts, cells_x, field_ref, tiles_ref, *refs):
    early_refs, (buffer, early, total, sems) = refs[:-4], refs[-4:]
    species = field_ref.shape[0]
    pitch = up(species, HALF_ROWS)
    spans = [slice(top, end) for top, end in zip(cuts[:-1], cuts[1:], strict=True)]
    copies = [
        pltpu.make_async_copy(field_ref.at[:, span, :], buffer.at[:, span, :], sems.at[i])
        for i, span in enumerate(spans)
    ]
    for copy in copies:
        copy.start()
    total[...] = jnp.zeros_like(total)
    sends = [
        pltpu.make_async_copy(early.at[k], ref, sems.at[len(copies) + k])
        for k, ref in enumerate(early_refs)
    ]
    for i, (copy, span) in enumerate(zip(copies, spans, strict=True)):
        copy.wait()
        for k, send in enumerate(sends if i == 0 else ()):
            early[k] = buffer[:, pl.ds(partner(partners(len(sends) + 1)[k + 1]), early.shape[2], stride=cells_x), :]
            send.start()
        both = stacked(buffer[:, span, :], pitch)
        total[: 2 * pitch, : 2 * pitch] += dot32(both, both, BY_LAST)
    upper = total[:pitch, :] + total[pitch : 2 * pitch, :]
    upper = upper + pltpu.roll(upper, LANES - pitch, 1)
    lane = lax.broadcasted_iota(jnp.int32, (ROWS, LANES), 1)
    tile = jnp.zeros((ROWS, LANES), jnp.float32)
    for top, at in triangle(species):
        moved = pltpu.roll(upper[top : top + ROWS, :], (at - top) % LANES, 1)
        tile = jnp.where((lane >= at) & (lane < at + species - top), moved, tile)
    tiles_ref[...] = jnp.broadcast_to(tile[None], tiles_ref.shape)
    for send in sends:
        send.wait()


def by_rows(field):
    species, cells_x, lines, cells = field.shape
    return field.transpose(0, 2, 1, 3).reshape(species, lines * cells_x, cells)


def gram_tiles(field, devices, early, count):
    species, cells_x, lines, cells = field.shape
    rows = lines * cells_x
    pitch = up(species, HALF_ROWS)
    cuts = (0, max(up(rows * 2 // 5, ROWS), early * cells_x), up(rows * 3 // 4, ROWS), rows)
    return pl.pallas_call(
        functools.partial(gram_kernel, cuts, cells_x),
        in_specs=[ANY],
        out_specs=[VMEM] + [ANY] * count,
        out_shape=[jax.ShapeDtypeStruct((devices, ROWS, LANES), jnp.float32)]
        + [jax.ShapeDtypeStruct((species, early, cells), jnp.float32)] * count,
        scratch_shapes=[
            pltpu.VMEM((species, rows, cells), jnp.float32),
            pltpu.VMEM((max(count, 1), species, max(early, ROWS), cells), jnp.float32),
            pltpu.VMEM((up(2 * pitch, LANES), LANES), jnp.float32),
            pltpu.SemaphoreType.DMA((len(cuts) - 1 + count,)),
        ],
        compiler_params=LARGE,
        name="gram_tiles",
    )(by_rows(field))


def orth(rows):
    ranks = rows.shape[0]
    blocks = ranks // ROWS
    rows = [rows[b * ROWS : (b + 1) * ROWS] for b in range(blocks)]
    shape = rows[0].shape
    index = lax.broadcasted_iota(jnp.int32, shape, 0)
    columns, pivots = [], []
    for k in range(ranks):
        row = rows[k // ROWS][k % ROWS : k % ROWS + 1, :]
        columns.append(
            {
                b: jnp.broadcast_to(jnp.sum(rows[b] * row, axis=1, keepdims=True), shape)
                for b in range(k // ROWS, blocks)
            }
        )
    for k in range(ranks):
        own, at = divmod(k, ROWS)
        pivot = columns[k][own][at : at + 1, :]
        below = {**columns[k], own: jnp.where(index > at, columns[k][own], 0.0)}
        inverse = 1.0 / pivot
        factor = {b: part * inverse for b, part in below.items()}
        if at == 0:
            pivots.append(jnp.broadcast_to(pivot, shape))
        pivots[own] = jnp.where(index == at, pivot, pivots[own])
        for j in range(k + 1, ranks):
            entry = columns[k][j // ROWS][j % ROWS : j % ROWS + 1, :]
            for b in columns[j]:
                columns[j][b] = columns[j][b] - factor[b] * entry
        row = rows[own][at : at + 1, :]
        for b in factor:
            rows[b] = rows[b] - factor[b] * row
    return jnp.concatenate([r * lax.rsqrt(p) for r, p in zip(rows, pivots, strict=True)], axis=0)


def start_kernel(start_ref, out_ref):
    out_ref[...] = orth(orth(start_ref[...]))


def unpacked(tile, species):
    parts = [pltpu.roll(tile, (top - at) % LANES, 1) for top, at in triangle(species)]
    parts += [jnp.zeros((ROWS, LANES), jnp.float32)] * (LANES // ROWS - len(parts))
    upper = jnp.concatenate(parts, axis=0)
    row = lax.broadcasted_iota(jnp.int32, (LANES, LANES), 0)
    column = lax.broadcasted_iota(jnp.int32, (LANES, LANES), 1)
    gram = jnp.where(column >= row // ROWS * ROWS, upper, upper.T)
    return jnp.where((row < species) & (column < species), gram, 0.0)


def turn(rows, gram):
    return orth(orth(jnp.dot(rows, gram, precision=HIGH, preferred_element_type=jnp.float32)))


def doubled(rows, pitch):
    high, low = split(rows[:, :pitch])
    both = jnp.concatenate([high, low], axis=0)
    return jnp.concatenate([both, both], axis=1)


def projected(left, stack):
    both = dot32(left, stack, PLAIN)
    ranks = left.shape[0] // 2
    return both[:ranks] + both[ranks:]


def whole_call(kernel, out_shape, name, *args):
    return pl.pallas_call(
        kernel, out_shape=out_shape, compiler_params=SMALL, cost_estimate=lasting(0), name=name
    )(*args)


def basis_kernel(species, scale, tiles_ref, start_ref, rows_ref, basis_ref):
    gram = unpacked(jnp.sum(tiles_ref[...], axis=0) * scale, species)
    rows = start_ref[...]
    for _ in range(ITERS):
        rows = turn(rows, gram)
    rows_ref[...] = rows
    basis_ref[...] = rows[:, :species]


def basis_late_kernel(scale, top, cells_x, tiles_ref, start_ref, field_ref, *refs):
    rows_ref, basis_ref = refs[:2]
    late_refs, core_ref = refs[2:-1], refs[-1]
    species, _, cells = field_ref.shape
    pitch = up(species, HALF_ROWS)
    gram = unpacked(jnp.sum(tiles_ref[...], axis=0) * scale, species)
    rows = start_ref[...]
    for _ in range(ITERS - 1):
        rows = turn(rows, gram)
    stack = stacked(field_ref[:, top:, :], pitch)
    rows = turn(rows, gram)
    rows_ref[...] = rows
    basis_ref[...] = rows[:, :species]
    core = projected(doubled(rows, pitch), stack)
    for i in range(core_ref.shape[0]):
        core_ref[i] = core[:, i * cells : (i + 1) * cells]
    for k, late_ref in zip(partners(len(late_refs)), late_refs, strict=True):
        for y in range(late_ref.shape[0]):
            late_ref[y] = core_ref[y * cells_x + partner(k)]


def basis_late(scale, early, count, tiles, first, field):
    species, cells_x, lines, cells = field.shape
    ranks = first.shape[0]
    late = lines - early
    return pl.pallas_call(
        functools.partial(basis_late_kernel, scale, early * cells_x, cells_x),
        in_specs=[VMEM, VMEM, VMEM],
        out_specs=[VMEM] * (2 + count),
        out_shape=[
            jax.ShapeDtypeStruct((ranks, LANES), jnp.float32),
            jax.ShapeDtypeStruct((ranks, species), jnp.float32),
        ]
        + [jax.ShapeDtypeStruct((late, ranks, cells), jnp.float32)] * count,
        scratch_shapes=[
            pltpu.VMEM((late * cells_x, ranks, cells), jnp.float32),
        ],
        compiler_params=MIDDLE,
        cost_estimate=lasting(30),
        name="basis_late",
    )(tiles, first, by_rows(field))


def place(core, at, high_ref, low_ref):
    lines, ranks, cells = core.shape
    block = core.reshape(lines, ranks * cells)
    if lines % HALF_ROWS:
        fill = jnp.zeros((up(lines, HALF_ROWS) - lines, ranks * cells), jnp.float32)
        block = jnp.concatenate([block, fill], axis=0)
    high, low = split(block)
    high_ref[pl.ds(at, block.shape[0]), :] = high
    low_ref[pl.ds(at, block.shape[0]), :] = low


def ready_kernel(cells_x, rows_ref, late_ref, field_ref, *refs):
    pieces, (high_ref, low_ref, part_ref) = refs[:-3], refs[-3:]
    size = len(pieces) + 1
    pitch = high_ref.shape[0] // size
    species, early, cells = pieces[0].shape
    wide = up(species, HALF_ROWS)
    left = doubled(rows_ref[...], wide)
    for i, k in enumerate(partners(size)):
        if k == 0:
            piece = field_ref[:, pl.ds(partner(0), early, stride=cells_x), :]
        else:
            piece = pieces[i - 1][...]
        core = projected(left, stacked(piece, wide))
        for y in range(early):
            part_ref[y] = core[:, y * cells : (y + 1) * cells]
        place(part_ref[...], pl.multiple_of(partner(k) * pitch, HALF_ROWS), high_ref, low_ref)
    at = pl.multiple_of(partner(0) * pitch + early, HALF_ROWS)
    place(late_ref[...], at, high_ref, low_ref)


def ready_rows(rows, own, field, pieces, lines):
    _, early, cells = pieces[0].shape
    ranks = rows.shape[0]
    shape = ((len(pieces) + 1) * up(lines, HALF_ROWS), ranks * cells)
    return pl.pallas_call(
        functools.partial(ready_kernel, field.shape[1]),
        in_specs=[VMEM] * (3 + len(pieces)),
        out_specs=[VMEM, VMEM],
        out_shape=[jax.ShapeDtypeStruct(shape, jnp.bfloat16)] * 2,
        scratch_shapes=[pltpu.VMEM((early, ranks, cells), jnp.float32)],
        compiler_params=PARAMS,
        name="ready_rows",
    )(rows, own, by_rows(field), *pieces)


def packing(lines, columns):
    groups = LANES // lines
    deep = -(-columns // groups)
    return groups, deep, up(deep, ROWS)


def line_kernel(axes, lines, early, count, *refs):
    n_gx, n_gy, n_sa = axes
    pieces, ready, (out_ref, high_ref, low_ref, gram_ref) = refs[:count], refs[count:-4], refs[-4:]
    pitch = high_ref.shape[0] // n_gy
    if ready:
        high_ref[...] = ready[0][...]
        low_ref[...] = ready[1][...]
    for k in range(count):
        block = partner(partners(n_gy)[n_gy - count + k])
        place(pieces[k][...], pl.multiple_of(block * pitch + early, HALF_ROWS), high_ref, low_ref)
    size = n_gy * pitch
    gram_ref[...] = jnp.zeros_like(gram_ref)
    gram_ref[:size, :size] = dot32(high_ref[...], low_ref[...], BY_LAST)
    cross = gram_ref[:size, :size]
    gram_ref[:size, :size] = dot32(high_ref[...], high_ref[...], BY_LAST) + cross + cross.T
    wide = gram_ref.shape[1]
    columns = lines * n_gy // (n_gx * n_sa)
    groups, deep, tall = packing(lines, columns)
    lane = lax.broadcasted_iota(jnp.int32, (tall, LANES), 1)
    for c in range(n_gx * n_sa):
        first = c * columns
        base = first // lines * pitch + first % lines
        bands = [gram_ref[base + g * deep : base + g * deep + tall, :] for g in range(groups)]
        for i in range(n_gy):
            tile = jnp.zeros((tall, LANES), jnp.float32)
            for g in range(groups):
                moved = pltpu.roll(bands[g], (g * lines - i * pitch) % wide, 1)[:, :LANES]
                tile = jnp.where((lane >= g * lines) & (lane < (g + 1) * lines), moved, tile)
            out_ref[((c // n_sa) * n_gy + i) * n_sa + c % n_sa] = tile


def line_tiles(pieces, ready, axes, lines, early):
    n_gx, n_gy, n_sa = axes
    _, ranks, cells = pieces[0].shape
    size = n_gy * up(lines, HALF_ROWS)
    _, _, tall = packing(lines, lines * n_gy // (n_gx * n_sa))
    return pl.pallas_call(
        functools.partial(line_kernel, axes, lines, early, len(pieces)),
        in_specs=[VMEM] * (len(pieces) + len(ready)),
        out_specs=VMEM,
        out_shape=jax.ShapeDtypeStruct((n_gx * n_gy * n_sa, tall, LANES), jnp.float32),
        scratch_shapes=[
            pltpu.VMEM((size, ranks * cells), jnp.bfloat16),
            pltpu.VMEM((size, ranks * cells), jnp.bfloat16),
            pltpu.VMEM((size + tall, up(size, LANES)), jnp.float32),
        ],
        compiler_params=PARAMS,
        name="line_tiles",
    )(*pieces, *ready)


def block_kernel(scale, tiles_ref, out_ref):
    columns, lines = out_ref.shape
    groups, deep, _ = packing(lines, columns)
    tile = jnp.sum(tiles_ref[...], axis=0) * scale
    for g in range(groups):
        part = tile if g == 0 else pltpu.roll(tile, LANES - g * lines, 1)
        high = min(deep, columns - g * deep)
        if high > 0:
            out_ref[g * deep : g * deep + high, :] = part[:high, :lines]


def partners(size):
    if size & (size - 1):
        raise ValueError("axis size")
    return sorted(range(size), key=lambda k: (k > 0, -k.bit_count(), -k))


def exchanges(pieces, size):
    return [
        lax.ppermute(piece, "gy", [(a, a ^ k) for a in range(size)])
        for k, piece in zip(partners(size)[1:], pieces, strict=True)
    ]


def on_device(field, start):
    species, cells_x, lines, cells_z = field.shape
    ranks = start.shape[1]
    n_gx, n_gy, n_sa = lax.axis_size("gx"), lax.axis_size("gy"), lax.axis_size("sa")
    axes, devices = (n_gx, n_gy, n_sa), n_gx * n_gy * n_sa
    total_x, total_y, total_z = cells_x * n_gx, lines * n_gy, cells_z * n_sa
    columns = total_y // (n_gx * n_sa)
    me = lax.axis_index("gy")
    parts_x = math.gcd(n_gy, cells_x)
    parts_z = n_gy // parts_x
    early = lines * 2 // 5 // HALF_ROWS * HALF_ROWS
    by_x = parts_x == cells_x and parts_z == 1 and early > 0
    early = early if by_x else 0

    tiles, *outgoing = gram_tiles(field, devices, early, n_gy - 1 if by_x else 0)
    tiles = lax.all_to_all(tiles, ALL, 0, 0, tiled=True)
    first = whole_call(
        start_kernel,
        jax.ShapeDtypeStruct((ranks, LANES), jnp.float32),
        "start_rows",
        jnp.pad(start.T, ((0, 0), (0, LANES - species))),
    )
    scale = 1.0 / (total_x * total_y * total_z)
    if by_x:
        received = exchanges(outgoing, n_gy)
        rows, basis, own, *pieces = basis_late(scale, early, n_gy, tiles, first, field)
        pieces = exchanges(pieces, n_gy)
        ready = ready_rows(rows, own, field, received, lines)
    else:
        rows, basis = whole_call(
            functools.partial(basis_kernel, species, scale),
            [
                jax.ShapeDtypeStruct((ranks, LANES), jnp.float32),
                jax.ShapeDtypeStruct((ranks, species), jnp.float32),
            ],
            "basis_rows",
            tiles,
            first,
        )
        wide_x, wide_z = cells_x // parts_x, cells_z // parts_z
        core = jnp.einsum("rs,sxyz->yrxz", rows[:, :species], field, precision=HIGH)
        pieces, ready = [], []
        for k in partners(n_gy):
            at = jnp.bitwise_xor(me, k)
            cut = lax.dynamic_slice(
                core,
                (0, 0, at // parts_z * wide_x, at % parts_z * wide_z),
                (lines, ranks, wide_x, wide_z),
            )
            pieces.append(cut.reshape(lines, -1, LANES))
        pieces = pieces[:1] + exchanges(pieces[1:], n_gy)
    blocks = line_tiles(pieces, ready, axes, lines, early)
    blocks = lax.all_to_all(blocks, ALL, 0, 0, tiled=True)
    block = whole_call(
        functools.partial(block_kernel, 1.0 / (ranks * total_x * total_z)),
        jax.ShapeDtypeStruct((columns, lines), jnp.float32),
        "own_block",
        blocks,
    )
    return (basis.T, block.T)


def solution(mesh):
    in_specs = (P(None, "gx", "gy", "sa"), P())
    out_specs = (P(), P("gy", ("gx", "sa")))
    return jax.shard_map(
        on_device, mesh=mesh, in_specs=in_specs, out_specs=out_specs, check_vma=False
    )
```
